512 devices in a mesh: tile: 128 (over z, x, y_lo), cls: 4 (over y_hi, core).
Axes of the slice: x: 4, y: 8 (y_hi: 2, y_lo: 4; y = y_hi * 4 + y_lo), z: 8, core: 2. Of those that a mesh axis runs over, the one named last changes fastest.
Arguments:
- concentration: float32 [64, 4, 262144], P('cls', None, 'tile'), may hold values from 0.05 to 2
- velocity: float32 [2, 4, 262144], P(None, None, 'tile'), may hold values from -0.3 to 0.3
- land_mask: int32 [262144], P('tile'), may hold values 0 or 1
- settling: float32 [64], P('cls'), may hold values from 0.01 to 0.3
- breakage_rate: float32 [64], replicated, may hold values from 0.02 to 0.3
- kernel_levels: int32 [64, 64], replicated, may hold values from 100 to 1000, as said below
- pair_target: int32 [64, 64], replicated, may hold values from 0 to 63, as said below
- fragment_weights: int32 [64, 64], replicated, may hold values from 1 to 16
Outputs:
- flocs: float32 [64, 4, 262144], P('cls', None, 'tile')
The draws below stay inside these ranges and needn't reach their ends.
Inputs may be any that keep to these rules, and one draw needn't show every extreme that they name: `kernel_levels`: symmetric. `pair_target`: symmetric, and entry [i, j] is at least the larger of i and j.
All inputs are finite; a program needn't handle non-finite values. No bound on the sum of `land_mask` on one device may be relied on, other than what follows from the above.
Results may differ from the reference program's by a relative error of at most 0.0001.
Values sent between devices are 32-bit elements; how exact they have to be, the bound alone decides.
No kernel may reach another device: no remote copies, remote signals or barrier semaphores. Data moves between devices by JAX's collectives and lax.ppermute only.
A program may use at most 64 MiB of HBM per device.

```python
import math
import jax
import jax.numpy as jnp
from jax import lax

NC = 64
L = 4
CY = 512
CX = 4
COLUMNS = 262144
N_TILE = 128


def draw_kernel_levels(key, part):
    half = jax.random.randint(jax.random.fold_in(key, 11), (NC, NC), 50, 501, dtype=jnp.int32)
    return (half + half.T).astype(jnp.int32)


def draw_pair_target(key, part):
    extra = jax.random.randint(jax.random.fold_in(key, 23), (NC, NC), 0, 2, dtype=jnp.int32)
    extra = extra + extra.T
    rank = jnp.arange(NC, dtype=jnp.int32)
    larger = jnp.maximum(rank[:, None], rank[None, :])
    return jnp.minimum(larger + extra, NC - 1).astype(jnp.int32)


def plant(values, key, low, top_value):
    index_at = [jax.random.randint(jax.random.fold_in(key, axis), (), 0, length) for axis, length in enumerate(values.shape)]
    longest = values.shape.index(max(values.shape))
    next_to = index_at[:longest] + [(index_at[longest] + 1) % values.shape[longest]] + index_at[longest + 1:]
    return values.at[tuple(index_at)].set(low).at[tuple(next_to)].set(top_value)


def block_levels(rng, dims, cuts, least, largest):
    loudness = 1.0
    for position, shards_of in cuts:
        heights = jax.random.uniform(jax.random.fold_in(jax.random.fold_in(rng, 6), position), (shards_of,), jnp.float32, least / len(cuts), largest / len(cuts))
        loudness = loudness * jnp.repeat(jnp.exp(heights), dims[position] // shards_of).reshape((-1,) + (1,) * (len(dims) - 1 - position))
    return loudness


def setup_inputs(seed: int = 0) -> dict:
    key_of = jax.random.split(jax.random.key(seed), 9)
    concentration = jnp.clip(jnp.exp(math.log(2.0) - 3.6888794 * jax.random.uniform(key_of[0], (NC, L, COLUMNS), jnp.float32) ** block_levels(key_of[0], (NC, L, COLUMNS), ((0, 4), (2, 128)), -0.2, 0.2)), 0.05, 2.0)
    velocity = jnp.clip(jax.random.uniform(key_of[1], (2, L, COLUMNS), jnp.float32, -0.3, 0.3) * block_levels(key_of[1], (2, L, COLUMNS), ((2, 128),), -0.4, 0.0), -0.3, 0.3)
    land_mask = plant((jax.random.randint(key_of[2], (COLUMNS,), 0, 8) < 7).astype(jnp.int32), jax.random.fold_in(key_of[2], 1), 0, 1)
    settling = jnp.clip(jnp.exp(math.log(0.3) - 3.4011974 * jax.random.uniform(key_of[3], (NC,), jnp.float32) ** block_levels(key_of[3], (NC,), ((0, 4),), -0.2, 0.2)), 0.01, 0.3)
    breakage_rate = jnp.clip(jnp.exp(jax.random.uniform(key_of[4], (NC,), jnp.float32, math.log(0.02), math.log(0.3))), 0.02, 0.3)
    kernel_levels = draw_kernel_levels(jax.random.fold_in(key_of[8], 71), 0)
    pair_target = draw_pair_target(jax.random.fold_in(key_of[8], 71), 0)
    fragment_weights = plant(jax.random.randint(key_of[7], (NC, NC), 1, 17), jax.random.fold_in(key_of[7], 1), 1, 16).astype(jnp.int32)
    return dict(concentration=concentration, velocity=velocity, land_mask=land_mask, settling=settling, breakage_rate=breakage_rate, kernel_levels=kernel_levels, pair_target=pair_target, fragment_weights=fragment_weights)


kernel_scale = 1e-5


def to_grid(array):
    lead = array.shape[:-1]
    return array.reshape(lead + (N_TILE * CX, CY))


def from_grid(array):
    lead = array.shape[:-2]
    return array.reshape(lead + (N_TILE * CX * CY,))


def face_flux(c_low, c_high, f_low, f_high, w_low, w_high):
    speed = 0.5 * (f_low + f_high) * w_low * w_high
    return jnp.maximum(speed, 0.0) * c_low + jnp.minimum(speed, 0.0) * c_high


def reference(concentration, velocity, land_mask, settling, breakage_rate, kernel_levels, pair_target, fragment_weights):
    field = to_grid(concentration)
    speeds = to_grid(velocity)
    water = to_grid(land_mask.astype(jnp.float32))
    cpad = jnp.pad(field, ((0, 0), (0, 0), (1, 1), (1, 1)))
    spad = jnp.pad(speeds, ((0, 0), (0, 0), (1, 1), (1, 1)))
    wpad = jnp.pad(water, ((1, 1), (1, 1)))
    fx = face_flux(cpad[:, :, :-1, 1:-1], cpad[:, :, 1:, 1:-1], spad[0, :, :-1, 1:-1], spad[0, :, 1:, 1:-1], wpad[:-1, 1:-1], wpad[1:, 1:-1])
    fy = face_flux(cpad[:, :, 1:-1, :-1], cpad[:, :, 1:-1, 1:], spad[1, :, 1:-1, :-1], spad[1, :, 1:-1, 1:], wpad[1:-1, :-1], wpad[1:-1, 1:])
    moved = field - (fx[:, :, 1:] - fx[:, :, :-1]) - (fy[:, :, :, 1:] - fy[:, :, :, :-1])
    sink = settling[:, None, None, None] * field
    moved = moved - sink + jnp.pad(sink[:, :-1], ((0, 0), (1, 0), (0, 0), (0, 0)))
    current = from_grid(moved).reshape(NC, -1)

    levels = kernel_levels.astype(jnp.float32) * kernel_scale
    rank = jnp.arange(NC, dtype=jnp.int32)
    hit = pair_target[None, :, :] == rank[:, None, None]
    birth = jnp.where(hit, 0.5 * levels[None, :, :], 0.0)
    lower = jnp.where(rank[:, None] <= rank[None, :], fragment_weights.astype(jnp.float32), 0.0)
    frag = lower / jnp.sum(lower, axis=0, keepdims=True)
    by_first = jnp.transpose(birth, (1, 0, 2))
    for sub in range(2):
        def add_pair(total, item):
            table, partner = item
            made = jnp.dot(table, current, precision=lax.Precision.HIGHEST, preferred_element_type=jnp.float32)
            return total + made * partner[None, :], None
        gain, _ = lax.scan(add_pair, jnp.zeros_like(current), (by_first, current))
        loss = current * jnp.dot(levels, current, precision=lax.Precision.HIGHEST, preferred_element_type=jnp.float32)
        broken = jnp.dot(frag, breakage_rate[:, None] * current, precision=lax.Precision.HIGHEST, preferred_element_type=jnp.float32) - breakage_rate[:, None] * current
        current = current + gain - loss + broken
    return current.reshape(NC, L, N_TILE * CX * CY)
```

```python
import jax
import jax.numpy as jnp
from jax import lax
from jax.experimental import pallas as pl
from jax.experimental.pallas import tpu as pltpu
from jax.sharding import PartitionSpec as P

CY = 512
CX = 4
LAYERS = 4
NC = 64
GROUP = 16
COLS = CX * CY
TILE = 256
HALF_SCALE = 0.5e-05
VMEM_LIMIT = 48 * 1024 * 1024

SPANS = [NC - 8 * b for b in range(NC // 8)]
STARTS = [8 * sum(SPANS[:b]) for b in range(NC // 8)]
PAIR_ROWS = 8 * sum(SPANS)


def split(x):
    high = x.astype(jnp.bfloat16)
    low = (x - high.astype(jnp.float32)).astype(jnp.bfloat16)
    return high, low


def table_kernel(levels_ref, target_ref, weights_ref, rate_ref, pair_ref, linear_ref):
    levels = levels_ref[...].astype(jnp.float32)
    row = lax.broadcasted_iota(jnp.int32, (NC, NC), 0)
    col = lax.broadcasted_iota(jnp.int32, (NC, NC), 1)
    double = 2.0 * levels
    high, low = [part.astype(jnp.float32) for part in split(double)]
    weight = jnp.where(col < row, 1.0, jnp.where(col == row, 0.5, 0.0))
    lost = jnp.concatenate([high, high, low, low], 1)
    born = lost * jnp.concatenate([weight] * 4, 1)
    target = jnp.concatenate([target_ref[...]] * 4, 1)
    for b in range(NC // 8):
        span = SPANS[b]
        klass = lax.broadcasted_iota(jnp.int32, (span, 4 * NC), 0) + 8 * b
        for two in range(4):
            rows = []
            for i in (8 * b + 2 * two, 8 * b + 2 * two + 1):
                gain = jnp.where(klass == target[i : i + 1], born[i : i + 1], 0.0)
                loss = jnp.where(klass == i, lost[i : i + 1], 0.0)
                rows.append(gain - loss)
            at = STARTS[b] + 2 * two * span
            pair_ref[at : at + 2 * span, :] = jnp.concatenate(rows, 0).astype(jnp.bfloat16)
    lower = jnp.where(row <= col, weights_ref[...].astype(jnp.float32), 0.0)
    rate = rate_ref[...]
    linear = lower / jnp.sum(lower, axis=0, keepdims=True) * rate
    linear = linear - jnp.where(row == col, rate, 0.0)
    high, low = split(linear)
    linear_ref[...] = jnp.concatenate([high, high, low, low], 1)


def make_tables(kernel_levels, pair_target, fragment_weights, breakage_rate):
    return pl.pallas_call(
        table_kernel,
        out_shape=(
            jax.ShapeDtypeStruct((PAIR_ROWS, 4 * NC), jnp.bfloat16),
            jax.ShapeDtypeStruct((NC, 4 * NC), jnp.bfloat16),
        ),
        compiler_params=pltpu.CompilerParams(vmem_limit_bytes=VMEM_LIMIT),
        name="tables",
    )(kernel_levels, pair_target, fragment_weights, breakage_rate.reshape(1, NC))


def transport_kernel(
    c_ref, velocity_ref, mask_ref, settling_ref, west_ref, east_ref, out_ref
):
    mask = mask_ref[...].astype(jnp.float32)
    water = jnp.concatenate([mask[q : q + 1] for q in range(COLS // 128)], 1)
    wide = jnp.concatenate(
        [west_ref[GROUP + 1, 0:1, :], water, east_ref[GROUP + 1, 0:1, :]], 1
    )
    both_x = 0.5 * wide[:, :-CY] * wide[:, CY:]
    place = lax.broadcasted_iota(jnp.int32, (1, COLS), 1)
    both_y = jnp.where(place % CY == 0, 0.0, 0.5 * water * pltpu.roll(water, 1, 1))
    eye = lax.broadcasted_iota(jnp.int32, (GROUP, GROUP), 0) == lax.broadcasted_iota(
        jnp.int32, (GROUP, GROUP), 1
    )
    sink = jnp.sum(jnp.where(eye, settling_ref[...], 0.0), axis=1, keepdims=True)
    above = None
    for layer in range(LAYERS):
        c = c_ref[:, layer, :]
        u = jnp.concatenate(
            [
                west_ref[GROUP, layer : layer + 1, :],
                velocity_ref[0, layer : layer + 1, :],
                east_ref[GROUP, layer : layer + 1, :],
            ],
            1,
        )
        face_x = (u[:, :-CY] + u[:, CY:]) * both_x
        plus_x, minus_x = jnp.maximum(face_x, 0.0), jnp.minimum(face_x, 0.0)
        v = velocity_ref[1, layer : layer + 1, :]
        face_y = (v + pltpu.roll(v, 1, 1)) * both_y
        plus_y, minus_y = jnp.maximum(face_y, 0.0), jnp.minimum(face_y, 0.0)
        to_north = pltpu.roll(plus_y, COLS - 1, 1)
        from_north = pltpu.roll(minus_y, COLS - 1, 1)
        keep = 1.0 - plus_x[:, CY:] + minus_x[:, :-CY] - to_north + minus_y
        west = jnp.concatenate([west_ref[:GROUP, layer, :], c[:, :-CY]], 1)
        east = jnp.concatenate([c[:, CY:], east_ref[:GROUP, layer, :]], 1)
        south = pltpu.roll(c, 1, 1)
        north = pltpu.roll(c, COLS - 1, 1)
        moved = (
            c * (keep - sink)
            + west * plus_x[:, :-CY]
            - east * minus_x[:, CY:]
            + south * plus_y
            - north * from_north
        )
        if above is not None:
            moved = moved + sink * above
        above = c
        out_ref[layer] = moved


def transport(concentration, velocity, land_mask, settling, west, east):
    return pl.pallas_call(
        transport_kernel,
        out_shape=jax.ShapeDtypeStruct((LAYERS, GROUP, COLS), jnp.float32),
        compiler_params=pltpu.CompilerParams(vmem_limit_bytes=VMEM_LIMIT),
        name="transport",
    )(
        concentration,
        velocity,
        land_mask.reshape(COLS // 128, 128),
        settling.reshape(1, GROUP),
        west,
        east,
    )


def react_kernel(x_ref, pair_ref, linear_ref, out_ref):
    width = x_ref.shape[1]

    def tile(index, carry):
        at = pl.ds(pl.multiple_of(index * TILE, TILE), TILE)
        n = x_ref[:, at]
        for _ in range(2):
            high, low = split(n)
            stack = jnp.concatenate([high, low, high, low], 0)
            total = [jnp.zeros((8, TILE), jnp.float32) for _ in range(NC // 8)]
            for b in range(NC // 8):
                span = SPANS[b]
                made = jnp.dot(
                    pair_ref[STARTS[b] : STARTS[b] + 8 * span, :],
                    stack,
                    preferred_element_type=jnp.float32,
                )
                for ii in range(8):
                    partner = n[8 * b + ii : 8 * b + ii + 1]
                    for g in range(b, NC // 8):
                        row = ii * span + 8 * (g - b)
                        total[g] = total[g] + made[row : row + 8] * partner
            linear = jnp.dot(linear_ref[...], stack, preferred_element_type=jnp.float32)
            n = n + (HALF_SCALE * jnp.concatenate(total, 0) + linear)
        out_ref[:, at] = n
        return carry

    lax.fori_loop(0, width // TILE, tile, 0)


def react(x, pairs, linear):
    return pl.pallas_call(
        react_kernel,
        out_shape=jax.ShapeDtypeStruct(x.shape, jnp.float32),
        compiler_params=pltpu.CompilerParams(vmem_limit_bytes=VMEM_LIMIT),
        name="react",
    )(x, pairs, linear)


def passed_along(x, by):
    length = lax.axis_size("tile")
    pairs = [(i, i + by) for i in range(length) if 0 <= i + by < length]
    return lax.ppermute(x, "tile", pairs)


def body(
    concentration,
    velocity,
    land_mask,
    settling,
    breakage_rate,
    kernel_levels,
    pair_target,
    fragment_weights,
):
    water = land_mask.astype(jnp.float32)

    def edge(at):
        cut = slice(at, at + CY)
        return jnp.concatenate(
            [
                concentration[:, :, cut],
                velocity[:1, :, cut],
                jnp.broadcast_to(water[cut], (1, LAYERS, CY)),
            ],
            0,
        )

    west = passed_along(edge(COLS - CY), 1)
    east = passed_along(edge(0), -1)
    pairs, linear = make_tables(kernel_levels, pair_target, fragment_weights, breakage_rate)
    moved = transport(concentration, velocity, land_mask, settling, west, east)
    whole = lax.all_to_all(moved, "cls", 0, 0, tiled=True).reshape(NC, COLS)
    done = react(whole, pairs, linear).reshape(LAYERS, GROUP, COLS)
    mine = lax.all_to_all(done, "cls", 0, 0, tiled=True)
    return jnp.transpose(mine, (1, 0, 2))


def solution(mesh):
    placed = (
        P("cls", None, "tile"),
        P(None, None, "tile"),
        P("tile"),
        P("cls"),
        P(),
        P(),
        P(),
        P(),
    )
    return jax.shard_map(
        body, mesh=mesh, in_specs=placed, out_specs=P("cls", None, "tile"), check_vma=False
    )
```

```python
import jax
import jax.numpy as jnp
from jax import lax
from jax.experimental import pallas as pl
from jax.experimental.pallas import tpu as pltpu
from jax.sharding import Mesh
from jax.sharding import PartitionSpec as P

CY = 512
CX = 4
LAYERS = 4
NC = 64
GROUP = 16
COLS = CX * CY
WIDTH = 2 * CY
TILE = 256
HALF_SCALE = 0.5e-05
VMEM_LIMIT = 48 * 1024 * 1024

BLOCKS = NC // 8
ALL_SPANS = [NC - 8 * b for b in range(BLOCKS)]
OWN_SPANS = [min(NC // 2, NC - 8 * b) for b in range(BLOCKS)]


def starts(spans):
    return [8 * sum(spans[:b]) for b in range(BLOCKS + 1)]


ALL_STARTS, OWN_STARTS = starts(ALL_SPANS), starts(OWN_SPANS)


def split(x):
    high = x.astype(jnp.bfloat16)
    low = (x - high.astype(jnp.float32)).astype(jnp.bfloat16)
    return high, low


def call(kernel, out_shape, name, scratch=(), limit=VMEM_LIMIT, cost=None, **specs):
    if cost is not None:
        cost = pl.CostEstimate(flops=cost, bytes_accessed=0, transcendentals=0)
    return pl.pallas_call(
        kernel,
        out_shape=out_shape,
        scratch_shapes=scratch,
        **specs,
        compiler_params=pltpu.CompilerParams(vmem_limit_bytes=limit),
        cost_estimate=cost,
        name=name,
    )


def f32(*shape):
    return jax.ShapeDtypeStruct(shape, jnp.float32)


def table_kernel(levels_ref, target_ref, weights_ref, rate_ref, all_ref, own_ref, linear_ref):
    far = lax.axis_index("far")
    levels = levels_ref[...].astype(jnp.float32)
    row = lax.broadcasted_iota(jnp.int32, (NC, NC), 0)
    col = lax.broadcasted_iota(jnp.int32, (NC, NC), 1)
    double = 2.0 * levels
    high, low = [part.astype(jnp.float32) for part in split(double)]
    weight = jnp.where(col < row, 1.0, jnp.where(col == row, 0.5, 0.0))
    lost = jnp.concatenate([high, high, low, low], 1)
    born = lost * jnp.concatenate([weight] * 4, 1)
    target = jnp.concatenate([target_ref[...]] * 4, 1)

    def rows_of(i, first, span):
        klass = lax.broadcasted_iota(jnp.int32, (span, 4 * NC), 0) + first
        gain = jnp.where(klass == target[i : i + 1], born[i : i + 1], 0.0)
        return gain - jnp.where(klass == i, lost[i : i + 1], 0.0)

    for b in range(BLOCKS):
        for i in range(8 * b, 8 * b + 8, 2):
            span = ALL_SPANS[b]
            rows = jnp.concatenate([rows_of(i, 8 * b, span), rows_of(i + 1, 8 * b, span)], 0)
            at = ALL_STARTS[b] + (i - 8 * b) * span
            all_ref[at : at + 2 * span, :] = rows.astype(jnp.bfloat16)
            span = OWN_SPANS[b]
            first = far * (NC // 2) + (NC // 2 - span)
            rows = jnp.concatenate([rows_of(i, first, span), rows_of(i + 1, first, span)], 0)
            at = OWN_STARTS[b] + (i - 8 * b) * span
            own_ref[at : at + 2 * span, :] = rows.astype(jnp.bfloat16)
    lower = jnp.where(row <= col, weights_ref[...].astype(jnp.float32), 0.0)
    rate = rate_ref[...]
    linear = lower / jnp.sum(lower, axis=0, keepdims=True) * rate
    linear = linear - jnp.where(row == col, rate, 0.0)
    high, low = split(linear)
    linear_ref[...] = jnp.concatenate([high, high, low, low], 1)


def make_tables(kernel_levels, pair_target, fragment_weights, breakage_rate):
    bf16 = jnp.bfloat16
    return call(
        table_kernel,
        (
            jax.ShapeDtypeStruct((ALL_STARTS[-1], 4 * NC), bf16),
            jax.ShapeDtypeStruct((OWN_STARTS[-1], 4 * NC), bf16),
            jax.ShapeDtypeStruct((NC, 4 * NC), bf16),
        ),
        "tables",
    )(kernel_levels, pair_target, fragment_weights, breakage_rate.reshape(1, NC))


def column(settling):
    eye = lax.broadcasted_iota(jnp.int32, (GROUP, GROUP), 0) == lax.broadcasted_iota(
        jnp.int32, (GROUP, GROUP), 1
    )
    return jnp.sum(jnp.where(eye, settling, 0.0), axis=1, keepdims=True)


def water_of(mask_ref):
    mask = mask_ref[...].astype(jnp.float32)
    return jnp.concatenate([mask[q : q + 1] for q in range(COLS // 128)], 1)


def advect(pick, sink, out_ref):
    water_west, water, water_east = pick("water", 0)
    width = water.shape[1]
    place = lax.broadcasted_iota(jnp.int32, (1, width), 1)
    half_west = 0.5 * water_west * water
    half_east = 0.5 * water * water_east
    half_y = jnp.where(place % CY == 0, 0.0, 0.5 * water * pltpu.roll(water, 1, 1))
    above = None
    near = lax.axis_index("near")
    for layer in range(LAYERS):
        west, c, east = pick("c", layer)
        u_west, u, u_east = pick("u", layer)
        v = pick("v", layer)
        low_x = (u_west + u) * half_west
        high_x = (u + u_east) * half_east
        low_y = (v + pltpu.roll(v, 1, 1)) * half_y
        plus_y, minus_y = jnp.maximum(low_y, 0.0), jnp.minimum(low_y, 0.0)
        plus_x, minus_x = jnp.maximum(low_x, 0.0), jnp.minimum(high_x, 0.0)
        to_north = pltpu.roll(plus_y, width - 1, 1)
        from_north = pltpu.roll(minus_y, width - 1, 1)
        keep = 1.0 - jnp.maximum(high_x, 0.0) + jnp.minimum(low_x, 0.0) - to_north + minus_y
        moved = (
            c * (keep - sink)
            + west * plus_x
            - east * minus_x
            + pltpu.roll(c, 1, 1) * plus_y
            - pltpu.roll(c, width - 1, 1) * from_north
        )
        if above is not None:
            moved = moved + sink * above
        above = c
        out_ref[(near + layer // 2) % 2, layer % 2] = moved


def inner_kernel(*refs):
    taken, made = refs[:4], refs[4:7]
    here, sems = refs[7:11], refs[11]
    copies = [
        pltpu.make_async_copy(src, dst, sems.at[k]) for k, (src, dst) in enumerate(zip(taken, here))
    ]
    for copy in copies:
        copy.start()
    for copy in copies:
        copy.wait()
    inner_rows(*here, *made)


def inner_rows(c_ref, velocity_ref, mask_ref, settling_ref, out_ref, *edge_refs):
    water = water_of(mask_ref)
    even = lax.axis_index("tile") % 2 == 0

    def rows(x):
        first, last = x[..., :CY], x[..., COLS - CY :]
        return jnp.where(even, last, first), jnp.where(even, first, last)

    for ref, c, u, w in zip(edge_refs, rows(c_ref[...]), rows(velocity_ref[0]), rows(water)):
        ref[:GROUP] = c
        ref[GROUP] = u
        ref[GROUP + 1] = jnp.broadcast_to(w, (LAYERS, CY))

    def three(x):
        return x[:, : 2 * CY], x[:, CY : 3 * CY], x[:, 2 * CY :]

    def pick(what, layer):
        if what == "water":
            return three(water)
        if what == "c":
            return three(c_ref[:, layer, :])
        if what == "u":
            return three(velocity_ref[0, layer : layer + 1, :])
        return velocity_ref[1, layer : layer + 1, CY : 3 * CY]

    advect(pick, column(settling_ref[...]), out_ref)


def outer_kernel(
    c_ref,
    velocity_ref,
    mask_ref,
    settling_ref,
    even_ref,
    odd_ref,
    inner_ref,
    peer_ref,
    out_ref,
    both_ref,
):
    both_ref[0] = inner_ref[0]
    both_ref[1] = peer_ref[...]
    water = water_of(mask_ref)
    even = lax.axis_index("tile") % 2 == 0
    west_ref = jnp.where(even, odd_ref[...], even_ref[...])
    east_ref = jnp.where(even, even_ref[...], odd_ref[...])

    def three(west, x, east):
        return (
            jnp.concatenate([west, x[:, 2 * CY : 3 * CY]], 1),
            jnp.concatenate([x[:, :CY], x[:, 3 * CY :]], 1),
            jnp.concatenate([x[:, CY : 2 * CY], east], 1),
        )

    def pick(what, layer):
        if what == "water":
            return three(west_ref[GROUP + 1, :1, :], water, east_ref[GROUP + 1, :1, :])
        if what == "c":
            return three(west_ref[:GROUP, layer, :], c_ref[:, layer, :], east_ref[:GROUP, layer, :])
        if what == "u":
            at = slice(layer, layer + 1)
            return three(west_ref[GROUP, at, :], velocity_ref[0, at, :], east_ref[GROUP, at, :])
        v = velocity_ref[1, layer : layer + 1, :]
        return jnp.concatenate([v[:, :CY], v[:, 3 * CY :]], 1)

    advect(pick, column(settling_ref[...]), out_ref)


def gains(n, stack, table_ref, spans, first, count):
    total = [jnp.zeros((8, TILE), jnp.float32) for _ in range(count // 8)]
    for b in range(BLOCKS):
        span = spans[b]
        made = jnp.dot(
            table_ref[first[b] : first[b + 1], :], stack, preferred_element_type=jnp.float32
        )
        skip = (count - span) // 8
        for ii in range(8):
            partner = n[8 * b + ii : 8 * b + ii + 1]
            for g in range(span // 8):
                row = ii * span + 8 * g
                total[skip + g] = total[skip + g] + made[row : row + 8] * partner
    return jnp.concatenate(total, 0)


def stack_of(n):
    high, low = split(n)
    return jnp.concatenate([high, low, high, low], 0)


def later_react_kernel(ours_ref, theirs_ref, all_ref, own_ref, linear_ref, _, *rest):
    react_kernel(ours_ref, theirs_ref, all_ref, own_ref, linear_ref, *rest)


def react_kernel(ours_ref, theirs_ref, all_ref, own_ref, linear_ref, keep_ref, send_ref, whole):
    far, near = lax.axis_index("far"), lax.axis_index("near")
    groups = [2 * f + n for f in (far, 1 - far) for n in (near, 1 - near)]
    parts = [ref.at[place] for ref in (ours_ref, theirs_ref) for place in range(2)]

    def tile(index, carry):
        slot = index // (WIDTH // TILE)
        at = pl.ds(pl.multiple_of((index % (WIDTH // TILE)) * TILE, TILE), TILE)
        for group, part in zip(groups, parts):
            whole[group] = part[slot, :, at]
        n = whole[...].reshape(NC, TILE)
        stack = stack_of(n)
        made = gains(n, stack, all_ref, ALL_SPANS, ALL_STARTS, NC)
        linear = jnp.dot(linear_ref[...], stack, preferred_element_type=jnp.float32)
        n = n + (HALF_SCALE * made + linear)
        stack = stack_of(n)
        made = gains(n, stack, own_ref, OWN_SPANS, OWN_STARTS, NC // 2)
        mine = linear_ref[pl.ds(pl.multiple_of(far * (NC // 2), NC // 2), NC // 2), :]
        linear = jnp.dot(mine, stack, preferred_element_type=jnp.float32)
        n = jnp.where(far == 0, n[: NC // 2], n[NC // 2 :]) + (HALF_SCALE * made + linear)
        keep_ref[slot, :, at] = jnp.where(near == 0, n[:GROUP], n[GROUP:])
        send_ref[slot, :, at] = jnp.where(near == 0, n[GROUP:], n[:GROUP])
        return carry

    lax.fori_loop(0, 2 * WIDTH // TILE, tile, 0)


def react(*arrays):
    half = f32(2, GROUP, WIDTH)
    return call(
        react_kernel if len(arrays) == 5 else later_react_kernel,
        (half, half),
        "react",
        scratch=[pltpu.VMEM((4, GROUP, TILE), jnp.float32)],
        cost=8_000_000_000,
        in_specs=[pl.BlockSpec(memory_space=pltpu.VMEM)] * 5
        + [pl.BlockSpec(memory_space=pl.ANY)] * (len(arrays) - 5),
    )(*arrays)


def lay_kernel(inner_ref, outer_ref, inner_peer_ref, outer_peer_ref, out_ref):
    near = lax.axis_index("near")
    for layer in range(LAYERS):
        slot = layer % 2
        mine = near == layer // 2
        inner = jnp.where(mine, inner_ref[slot], inner_peer_ref[slot])
        outer = jnp.where(mine, outer_ref[slot], outer_peer_ref[slot])
        out_ref[:, layer, :] = jnp.concatenate([outer[:, :CY], inner, outer[:, CY:]], 1)


def swapped_in_pairs(x, first):
    length = lax.axis_size("tile")
    pairs = [(i, i + 1) for i in range(first, length - 1, 2)]
    return lax.ppermute(x, "tile", pairs + [(b, a) for a, b in pairs])


def swapped(x, axis):
    return lax.ppermute(x, axis, [(0, 1), (1, 0)])


def body(
    concentration,
    velocity,
    land_mask,
    settling,
    breakage_rate,
    kernel_levels,
    pair_target,
    fragment_weights,
):
    local = (
        concentration,
        velocity,
        land_mask.reshape(COLS // 128, 128),
        settling.reshape(1, GROUP),
    )
    halves = f32(2, 2, GROUP, WIDTH)
    edge = f32(GROUP + 2, LAYERS, CY)
    inner, to_even, to_odd = call(
        inner_kernel,
        (halves, edge, edge),
        "inner",
        scratch=[pltpu.VMEM(x.shape, x.dtype) for x in local] + [pltpu.SemaphoreType.DMA((4,))],
        cost=1_000_000_000,
        in_specs=[pl.BlockSpec(memory_space=pltpu.HBM)] * 4,
    )(*[pltpu.with_memory_space_constraint(x, pltpu.HBM) for x in local])
    from_odd, from_even = swapped_in_pairs(to_odd, 1), swapped_in_pairs(to_even, 0)
    peer = swapped(inner[1], "near")
    tables = make_tables(kernel_levels, pair_target, fragment_weights, breakage_rate)
    outer, inner = call(outer_kernel, (halves, halves), "outer", cost=1_000_000_000)(
        *local, from_even, from_odd, inner, peer
    )
    inner_far = swapped(inner, "far")
    outer = jnp.concatenate([outer[:1], swapped(outer[1:], "near")], 0)
    outer_far = swapped(outer, "far")
    inner, inner_send = react(inner, inner_far, *tables, outer)
    outer, outer_send = react(outer, outer_far, *tables)
    inner_peer, outer_peer = swapped(inner_send, "near"), swapped(outer_send, "near")
    return call(lay_kernel, f32(GROUP, LAYERS, COLS), "lay")(inner, outer, inner_peer, outer_peer)


def solution(mesh):
    finer = Mesh(mesh.devices.reshape(mesh.shape["tile"], 2, 2), ("tile", "far", "near"))
    cls = ("far", "near")
    placed = (
        P(cls, None, "tile"),
        P(None, None, "tile"),
        P("tile"),
        P(cls),
        P(),
        P(),
        P(),
        P(),
    )
    return jax.shard_map(
        body, mesh=finer, in_specs=placed, out_specs=P(cls, None, "tile"), check_vma=False
    )
```

```python
import jax
import jax.numpy as jnp
from jax import lax
from jax.experimental import pallas as pl
from jax.experimental.pallas import tpu as pltpu
from jax.sharding import Mesh
from jax.sharding import PartitionSpec as P

CY = 512
CX = 4
LAYERS = 4
NC = 64
GROUP = 16
COLS = CX * CY
WIDTH = 2 * CY
TILE = 512
LANES = 4
DOTS = [[0, 1], [2, 3], [4, 5, 6, 7]]
HALF_SCALE = 0.5e-05
VMEM_LIMIT = 48 * 1024 * 1024

BLOCKS = NC // 8
ALL_SPANS = [NC - 8 * b for b in range(BLOCKS)]
OWN_SPANS = [min(NC // 2, NC - 8 * b) for b in range(BLOCKS)]


def starts(spans):
    return [8 * sum(spans[:b]) for b in range(BLOCKS + 1)]


ALL_STARTS, OWN_STARTS = starts(ALL_SPANS), starts(OWN_SPANS)


def split(x):
    high = x.astype(jnp.bfloat16)
    low = (x - high.astype(jnp.float32)).astype(jnp.bfloat16)
    return high, low


def call(kernel, out_shape, name, scratch=(), limit=VMEM_LIMIT, cost=None, **specs):
    if cost is not None:
        cost = pl.CostEstimate(flops=cost, bytes_accessed=0, transcendentals=0)
    return pl.pallas_call(
        kernel,
        out_shape=out_shape,
        scratch_shapes=scratch,
        **specs,
        compiler_params=pltpu.CompilerParams(vmem_limit_bytes=limit),
        cost_estimate=cost,
        name=name,
    )


def f32(*shape):
    return jax.ShapeDtypeStruct(shape, jnp.float32)


def table_kernel(levels_ref, target_ref, weights_ref, rate_ref, all_ref, own_ref, linear_ref):
    far = lax.axis_index("far")
    levels = levels_ref[...].astype(jnp.float32)
    row = lax.broadcasted_iota(jnp.int32, (NC, NC), 0)
    col = lax.broadcasted_iota(jnp.int32, (NC, NC), 1)
    double = 2.0 * levels
    high, low = [part.astype(jnp.float32) for part in split(double)]
    weight = jnp.where(col < row, 1.0, jnp.where(col == row, 0.5, 0.0))
    lost = jnp.concatenate([high, high, low, low], 1)
    born = lost * jnp.concatenate([weight] * 4, 1)
    target = jnp.concatenate([target_ref[...]] * 4, 1)

    def rows_of(i, first, span):
        klass = lax.broadcasted_iota(jnp.int32, (span, 4 * NC), 0) + first
        gain = jnp.where(klass == target[i : i + 1], born[i : i + 1], 0.0)
        return gain - jnp.where(klass == i, lost[i : i + 1], 0.0)

    for b in range(BLOCKS):
        for i in range(8 * b, 8 * b + 8, 2):
            span = ALL_SPANS[b]
            rows = jnp.concatenate([rows_of(i, 8 * b, span), rows_of(i + 1, 8 * b, span)], 0)
            at = ALL_STARTS[b] + (i - 8 * b) * span
            all_ref[at : at + 2 * span, :] = rows.astype(jnp.bfloat16)
            span = OWN_SPANS[b]
            first = far * (NC // 2) + (NC // 2 - span)
            rows = jnp.concatenate([rows_of(i, first, span), rows_of(i + 1, first, span)], 0)
            at = OWN_STARTS[b] + (i - 8 * b) * span
            own_ref[at : at + 2 * span, :] = rows.astype(jnp.bfloat16)
    lower = jnp.where(row <= col, weights_ref[...].astype(jnp.float32), 0.0)
    rate = rate_ref[...]
    linear = lower / jnp.sum(lower, axis=0, keepdims=True) * rate
    linear = linear - jnp.where(row == col, rate, 0.0)
    high, low = split(linear)
    linear_ref[...] = jnp.concatenate([high, high, low, low], 1)


def make_tables(kernel_levels, pair_target, fragment_weights, breakage_rate):
    bf16 = jnp.bfloat16
    return call(
        table_kernel,
        (
            jax.ShapeDtypeStruct((ALL_STARTS[-1], 4 * NC), bf16),
            jax.ShapeDtypeStruct((OWN_STARTS[-1], 4 * NC), bf16),
            jax.ShapeDtypeStruct((NC, 4 * NC), bf16),
        ),
        "tables",
    )(kernel_levels, pair_target, fragment_weights, breakage_rate.reshape(1, NC))


def column(settling):
    eye = lax.broadcasted_iota(jnp.int32, (GROUP, GROUP), 0) == lax.broadcasted_iota(
        jnp.int32, (GROUP, GROUP), 1
    )
    return jnp.sum(jnp.where(eye, settling, 0.0), axis=1, keepdims=True)


def water_of(mask_ref):
    mask = mask_ref[...].astype(jnp.float32)
    return jnp.concatenate([mask[q : q + 1] for q in range(COLS // 128)], 1)


def advect(pick, sink, out_ref):
    water_west, water, water_east = pick("water", 0)
    width = water.shape[1]
    place = lax.broadcasted_iota(jnp.int32, (1, width), 1)
    half_west = 0.5 * water_west * water
    half_east = 0.5 * water * water_east
    half_y = jnp.where(place % CY == 0, 0.0, 0.5 * water * pltpu.roll(water, 1, 1))
    above = None
    near = lax.axis_index("near")
    for layer in range(LAYERS):
        west, c, east = pick("c", layer)
        u_west, u, u_east = pick("u", layer)
        v = pick("v", layer)
        low_x = (u_west + u) * half_west
        high_x = (u + u_east) * half_east
        low_y = (v + pltpu.roll(v, 1, 1)) * half_y
        plus_y, minus_y = jnp.maximum(low_y, 0.0), jnp.minimum(low_y, 0.0)
        plus_x, minus_x = jnp.maximum(low_x, 0.0), jnp.minimum(high_x, 0.0)
        to_north = pltpu.roll(plus_y, width - 1, 1)
        from_north = pltpu.roll(minus_y, width - 1, 1)
        keep = 1.0 - jnp.maximum(high_x, 0.0) + jnp.minimum(low_x, 0.0) - to_north + minus_y
        moved = (
            c * (keep - sink)
            + west * plus_x
            - east * minus_x
            + pltpu.roll(c, 1, 1) * plus_y
            - pltpu.roll(c, width - 1, 1) * from_north
        )
        if above is not None:
            moved = moved + sink * above
        above = c
        out_ref[(near + layer // 2) % 2, layer % 2] = moved


def fetched(pairs, sems):
    copies = [pltpu.make_async_copy(*pair, sems.at[k]) for k, pair in enumerate(pairs)]
    for copy in copies:
        copy.start()
    for copy in copies:
        copy.wait()


def edge_kernel(c_ref, velocity_ref, mask_ref, to_even_ref, to_odd_ref, mask, u, sems):
    even = lax.axis_index("tile") % 2
    ends = [pl.ds(pl.multiple_of(at * (COLS - CY), CY), CY) for at in (1 - even, even)]
    outs = (to_even_ref, to_odd_ref)
    pairs = [(mask_ref, mask), (velocity_ref.at[0], u)]
    pairs += [(c_ref.at[:, :, end], out.at[:GROUP]) for end, out in zip(ends, outs)]
    fetched(pairs, sems)
    water = water_of(mask)
    for out, last in zip(outs, (even == 0, even != 0)):
        out[GROUP] = jnp.where(last, u[:, COLS - CY :], u[:, :CY])
        w = jnp.where(last, water[:, COLS - CY :], water[:, :CY])
        out[GROUP + 1] = jnp.broadcast_to(w, (LAYERS, CY))


def inner_kernel(*refs):
    fetched(zip(refs[:4], refs[5:9]), refs[9])
    inner_rows(*refs[5:9], refs[4])


def inner_rows(c_ref, velocity_ref, mask_ref, settling_ref, out_ref):
    water = water_of(mask_ref)

    def three(x):
        return x[:, : 2 * CY], x[:, CY : 3 * CY], x[:, 2 * CY :]

    def pick(what, layer):
        if what == "water":
            return three(water)
        if what == "c":
            return three(c_ref[:, layer, :])
        if what == "u":
            return three(velocity_ref[0, layer : layer + 1, :])
        return velocity_ref[1, layer : layer + 1, CY : 3 * CY]

    advect(pick, column(settling_ref[...]), out_ref)


def outer_kernel(
    c_ref,
    velocity_ref,
    mask_ref,
    settling_ref,
    even_ref,
    odd_ref,
    inner_ref,
    peer_ref,
    out_ref,
    both_ref,
):
    both_ref[0] = inner_ref[0]
    both_ref[1] = peer_ref[...]
    water = water_of(mask_ref)
    even = lax.axis_index("tile") % 2 == 0
    west_ref = jnp.where(even, odd_ref[...], even_ref[...])
    east_ref = jnp.where(even, even_ref[...], odd_ref[...])

    def three(west, x, east):
        return (
            jnp.concatenate([west, x[:, 2 * CY : 3 * CY]], 1),
            jnp.concatenate([x[:, :CY], x[:, 3 * CY :]], 1),
            jnp.concatenate([x[:, CY : 2 * CY], east], 1),
        )

    def pick(what, layer):
        if what == "water":
            return three(west_ref[GROUP + 1, :1, :], water, east_ref[GROUP + 1, :1, :])
        if what == "c":
            return three(west_ref[:GROUP, layer, :], c_ref[:, layer, :], east_ref[:GROUP, layer, :])
        if what == "u":
            at = slice(layer, layer + 1)
            return three(west_ref[GROUP, at, :], velocity_ref[0, at, :], east_ref[GROUP, at, :])
        v = velocity_ref[1, layer : layer + 1, :]
        return jnp.concatenate([v[:, :CY], v[:, 3 * CY :]], 1)

    advect(pick, column(settling_ref[...]), out_ref)


def gains(n, stack, table_ref, spans, first, count):
    total = [jnp.zeros((8, TILE), jnp.float32) for _ in range(count // 8)]
    for blocks in DOTS:
        base = first[blocks[0]]
        made = jnp.dot(
            table_ref[base : first[blocks[-1] + 1], :], stack, preferred_element_type=jnp.float32
        )
        for b in blocks:
            span = spans[b]
            skip = (count - span) // 8
            for ii in range(8):
                partner = n[8 * b + ii : 8 * b + ii + 1]
                for g in range(span // 8):
                    row = first[b] - base + ii * span + 8 * g
                    total[skip + g] = total[skip + g] + made[row : row + 8] * partner
    return jnp.concatenate(total, 0)


def stack_of(n):
    high, low = split(n)
    return jnp.concatenate([high, low, high, low], 0)


def react_kernel(ours_ref, theirs_ref, all_ref, own_ref, linear_ref, *rest):
    keep_ref, send_ref, whole = rest[-3:]
    lanes = whole.shape[0]
    layers = ours_ref.shape[1]
    filled = 0
    if send_ref.shape[0] > layers:
        for ref in rest[:-3]:
            send_ref[filled : filled + ref.shape[0]] = ref[...]
            filled += ref.shape[0]
    far, near = lax.axis_index("far"), lax.axis_index("near")
    groups = [2 * f + n for f in (far, 1 - far) for n in (near, 1 - near)]
    parts = [ref.at[place] for ref in (ours_ref, theirs_ref) for place in range(2)]

    def step(index, carry):
        places = []
        for k in range(lanes):
            at = index * lanes + k
            slot = at // (WIDTH // TILE)
            places.append((slot, pl.ds(pl.multiple_of((at % (WIDTH // TILE)) * TILE, TILE), TILE)))
        ns = []
        for k, (slot, at) in enumerate(places):
            for group, part in zip(groups, parts):
                whole[k, group] = part[slot, :, at]
            ns.append(whole[k].reshape(NC, TILE))
        stacks = [stack_of(n) for n in ns]
        mades = [gains(*both, all_ref, ALL_SPANS, ALL_STARTS, NC) for both in zip(ns, stacks)]
        linears = [
            jnp.dot(linear_ref[...], stack, preferred_element_type=jnp.float32) for stack in stacks
        ]
        ns = [n + (HALF_SCALE * made + linear) for n, made, linear in zip(ns, mades, linears)]
        stacks = [stack_of(n) for n in ns]
        mades = [gains(*both, own_ref, OWN_SPANS, OWN_STARTS, NC // 2) for both in zip(ns, stacks)]
        mine = linear_ref[pl.ds(pl.multiple_of(far * (NC // 2), NC // 2), NC // 2), :]
        linears = [
            jnp.dot(mine, stack, preferred_element_type=jnp.float32) for stack in stacks
        ]
        for n, made, linear, (slot, at) in zip(ns, mades, linears, places):
            n = jnp.where(far == 0, n[: NC // 2], n[NC // 2 :]) + (HALF_SCALE * made + linear)
            keep_ref[slot, :, at] = jnp.where(near == 0, n[:GROUP], n[GROUP:])
            send_ref[filled + slot, :, at] = jnp.where(near == 0, n[GROUP:], n[:GROUP])
        return carry

    lax.fori_loop(0, layers * WIDTH // (lanes * TILE), step, 0)


def react(ours, theirs, tables, later=(), earlier=()):
    layers = ours.shape[1]
    sent = layers + sum(x.shape[0] for x in earlier)
    return call(
        react_kernel,
        (f32(layers, GROUP, WIDTH), f32(sent, GROUP, WIDTH)),
        "react",
        scratch=[pltpu.VMEM((min(LANES, layers * WIDTH // TILE), 4, GROUP, TILE), jnp.float32)],
        cost=3_000_000_000 * layers,
        in_specs=[pl.BlockSpec(memory_space=pltpu.VMEM)] * (5 + len(earlier))
        + [pl.BlockSpec(memory_space=pl.ANY)] * len(later),
    )(ours, theirs, *tables, *earlier, *later)


def lay_kernel(inner_ref, first_ref, second_ref, peer_ref, out_ref):
    near = lax.axis_index("near")
    outer_refs = (first_ref, second_ref)
    for layer in range(LAYERS):
        slot = layer % 2
        mine = near == layer // 2
        inner = jnp.where(mine, inner_ref[slot], peer_ref[slot])
        outer = jnp.where(mine, outer_refs[slot][0], peer_ref[2 + slot])
        out_ref[:, layer, :] = jnp.concatenate([outer[:, :CY], inner, outer[:, CY:]], 1)


def swapped_in_pairs(x, first):
    length = lax.axis_size("tile")
    pairs = [(i, i + 1) for i in range(first, length - 1, 2)]
    return lax.ppermute(x, "tile", pairs + [(b, a) for a, b in pairs])


def swapped(x, axis):
    return lax.ppermute(x, axis, [(0, 1), (1, 0)])


def body(
    concentration,
    velocity,
    land_mask,
    settling,
    breakage_rate,
    kernel_levels,
    pair_target,
    fragment_weights,
):
    local = (
        concentration,
        velocity,
        land_mask.reshape(COLS // 128, 128),
        settling.reshape(1, GROUP),
    )
    halves = f32(2, 2, GROUP, WIDTH)
    edge = f32(GROUP + 2, LAYERS, CY)
    placed = [pltpu.with_memory_space_constraint(x, pltpu.HBM) for x in local]
    to_even, to_odd = call(
        edge_kernel,
        (edge, edge),
        "edges",
        scratch=[
            pltpu.VMEM(local[2].shape, jnp.int32),
            pltpu.VMEM((LAYERS, COLS), jnp.float32),
            pltpu.SemaphoreType.DMA((4,)),
        ],
        in_specs=[pl.BlockSpec(memory_space=pltpu.HBM)] * 3,
    )(*placed[:3])
    from_odd, from_even = swapped_in_pairs(to_odd, 1), swapped_in_pairs(to_even, 0)
    inner = call(
        inner_kernel,
        halves,
        "inner",
        scratch=[pltpu.VMEM(x.shape, x.dtype) for x in local] + [pltpu.SemaphoreType.DMA((4,))],
        in_specs=[pl.BlockSpec(memory_space=pltpu.HBM)] * 4,
    )(*placed)
    peer = swapped(inner[1], "near")
    tables = make_tables(kernel_levels, pair_target, fragment_weights, breakage_rate)
    outer, inner = call(outer_kernel, (halves, halves), "outer", cost=1_000_000_000)(
        *local, from_even, from_odd, inner, peer
    )
    inner_far = swapped(inner, "far")
    outer_peer = swapped(outer[1:], "near")
    ours = [jnp.concatenate([outer[:1, k : k + 1], outer_peer[:, k : k + 1]], 0) for k in range(2)]
    theirs = [swapped(x, "far") for x in ours]
    inner, sent = react(inner, inner_far, tables, later=ours)
    first, sent_first = react(ours[0], theirs[0], tables)
    second, sent = react(ours[1], theirs[1], tables, earlier=(sent, sent_first))
    peer = swapped(sent, "near")
    return call(lay_kernel, f32(GROUP, LAYERS, COLS), "lay")(inner, first, second, peer)


def solution(mesh):
    finer = Mesh(mesh.devices.reshape(mesh.shape["tile"], 2, 2), ("tile", "far", "near"))
    cls = ("far", "near")
    placed = (
        P(cls, None, "tile"),
        P(None, None, "tile"),
        P("tile"),
        P(cls),
        P(),
        P(),
        P(),
        P(),
    )
    return jax.shard_map(
        body, mesh=finer, in_specs=placed, out_specs=P(cls, None, "tile"), check_vma=False
    )
```

```python
import jax
import jax.numpy as jnp
from jax import lax
from jax.experimental import pallas as pl
from jax.experimental.pallas import tpu as pltpu
from jax.sharding import Mesh
from jax.sharding import PartitionSpec as P

CY = 512
CX = 4
LAYERS = 4
NC = 64
GROUP = 16
COLS = CX * CY
WIDTH = 2 * CY
TILE = 512
LANES = 4
DOTS = [[0, 1], [2, 3], [4, 5, 6, 7]]
HALF_SCALE = 0.5e-05
VMEM_LIMIT = 48 * 1024 * 1024

BLOCKS = NC // 8
ALL_SPANS = [NC - 8 * b for b in range(BLOCKS)]
OWN_SPANS = [min(NC // 2, NC - 8 * b) for b in range(BLOCKS)]


def starts(spans):
    return [8 * sum(spans[:b]) for b in range(BLOCKS + 1)]


ALL_STARTS, OWN_STARTS = starts(ALL_SPANS), starts(OWN_SPANS)


def split(x):
    high = x.astype(jnp.bfloat16)
    low = (x - high.astype(jnp.float32)).astype(jnp.bfloat16)
    return high, low


def call(kernel, out_shape, name, scratch=(), limit=VMEM_LIMIT, cost=None, **specs):
    if cost is not None:
        cost = pl.CostEstimate(flops=cost, bytes_accessed=0, transcendentals=0)
    return pl.pallas_call(
        kernel,
        out_shape=out_shape,
        scratch_shapes=scratch,
        **specs,
        compiler_params=pltpu.CompilerParams(vmem_limit_bytes=limit),
        cost_estimate=cost,
        name=name,
    )


def f32(*shape):
    return jax.ShapeDtypeStruct(shape, jnp.float32)


def table_kernel(levels_ref, target_ref, weights_ref, rate_ref, _, all_ref, own_ref, linear_ref):
    far = lax.axis_index("far")
    levels = levels_ref[...].astype(jnp.float32)
    row = lax.broadcasted_iota(jnp.int32, (NC, NC), 0)
    col = lax.broadcasted_iota(jnp.int32, (NC, NC), 1)
    double = 2.0 * levels
    high, low = [part.astype(jnp.float32) for part in split(double)]
    weight = jnp.where(col < row, 1.0, jnp.where(col == row, 0.5, 0.0))
    lost = jnp.concatenate([high, high, low, low], 1)
    born = lost * jnp.concatenate([weight] * 4, 1)
    target = jnp.concatenate([target_ref[...]] * 4, 1)

    def rows_of(i, first, span):
        klass = lax.broadcasted_iota(jnp.int32, (span, 4 * NC), 0) + first
        gain = jnp.where(klass == target[i : i + 1], born[i : i + 1], 0.0)
        return gain - jnp.where(klass == i, lost[i : i + 1], 0.0)

    for b in range(BLOCKS):
        for i in range(8 * b, 8 * b + 8, 2):
            span = ALL_SPANS[b]
            rows = jnp.concatenate([rows_of(i, 8 * b, span), rows_of(i + 1, 8 * b, span)], 0)
            at = ALL_STARTS[b] + (i - 8 * b) * span
            all_ref[at : at + 2 * span, :] = rows.astype(jnp.bfloat16)
            span = OWN_SPANS[b]
            first = far * (NC // 2) + (NC // 2 - span)
            rows = jnp.concatenate([rows_of(i, first, span), rows_of(i + 1, first, span)], 0)
            at = OWN_STARTS[b] + (i - 8 * b) * span
            own_ref[at : at + 2 * span, :] = rows.astype(jnp.bfloat16)
    lower = jnp.where(row <= col, weights_ref[...].astype(jnp.float32), 0.0)
    rate = rate_ref[...]
    linear = lower / jnp.sum(lower, axis=0, keepdims=True) * rate
    linear = linear - jnp.where(row == col, rate, 0.0)
    high, low = split(linear)
    linear_ref[...] = jnp.concatenate([high, high, low, low], 1)


def make_tables(kernel_levels, pair_target, fragment_weights, breakage_rate, after):
    bf16 = jnp.bfloat16
    return call(
        table_kernel,
        (
            jax.ShapeDtypeStruct((ALL_STARTS[-1], 4 * NC), bf16),
            jax.ShapeDtypeStruct((OWN_STARTS[-1], 4 * NC), bf16),
            jax.ShapeDtypeStruct((NC, 4 * NC), bf16),
        ),
        "tables",
        in_specs=[pl.BlockSpec(memory_space=pltpu.VMEM)] * 4
        + [pl.BlockSpec(memory_space=pl.ANY)],
    )(kernel_levels, pair_target, fragment_weights, breakage_rate.reshape(1, NC), after)


def column(settling):
    eye = lax.broadcasted_iota(jnp.int32, (GROUP, GROUP), 0) == lax.broadcasted_iota(
        jnp.int32, (GROUP, GROUP), 1
    )
    return jnp.sum(jnp.where(eye, settling, 0.0), axis=1, keepdims=True)


def water_of(mask_ref):
    mask = mask_ref[...].astype(jnp.float32)
    return jnp.concatenate([mask[q : q + 1] for q in range(COLS // 128)], 1)


def advect(pick, sink, out_ref):
    water_west, water, water_east = pick("water", 0)
    width = water.shape[1]
    place = lax.broadcasted_iota(jnp.int32, (1, width), 1)
    half_west = 0.5 * water_west * water
    half_east = 0.5 * water * water_east
    half_y = jnp.where(place % CY == 0, 0.0, 0.5 * water * pltpu.roll(water, 1, 1))
    above = None
    near = lax.axis_index("near")
    for layer in range(LAYERS):
        west, c, east = pick("c", layer)
        u_west, u, u_east = pick("u", layer)
        v = pick("v", layer)
        low_x = (u_west + u) * half_west
        high_x = (u + u_east) * half_east
        low_y = (v + pltpu.roll(v, 1, 1)) * half_y
        plus_y, minus_y = jnp.maximum(low_y, 0.0), jnp.minimum(low_y, 0.0)
        plus_x, minus_x = jnp.maximum(low_x, 0.0), jnp.minimum(high_x, 0.0)
        to_north = pltpu.roll(plus_y, width - 1, 1)
        from_north = pltpu.roll(minus_y, width - 1, 1)
        keep = 1.0 - jnp.maximum(high_x, 0.0) + jnp.minimum(low_x, 0.0) - to_north + minus_y
        moved = (
            c * (keep - sink)
            + west * plus_x
            - east * minus_x
            + pltpu.roll(c, 1, 1) * plus_y
            - pltpu.roll(c, width - 1, 1) * from_north
        )
        if above is not None:
            moved = moved + sink * above
        above = c
        out_ref[(near + layer // 2) % 2, layer % 2] = moved


def fetched(pairs, sems):
    copies = [pltpu.make_async_copy(*pair, sems.at[k]) for k, pair in enumerate(pairs)]
    for copy in copies:
        copy.start()
    for copy in copies:
        copy.wait()


def edge_kernel(c_ref, velocity_ref, mask_ref, to_even_ref, to_odd_ref, mask, u, sems):
    even = lax.axis_index("tile") % 2
    ends = [pl.ds(pl.multiple_of(at * (COLS - CY), CY), CY) for at in (1 - even, even)]
    outs = (to_even_ref, to_odd_ref)
    pairs = [(mask_ref, mask), (velocity_ref.at[0], u)]
    pairs += [(c_ref.at[:, :, end], out.at[:GROUP]) for end, out in zip(ends, outs)]
    fetched(pairs, sems)
    water = water_of(mask)
    for out, last in zip(outs, (even == 0, even != 0)):
        out[GROUP] = jnp.where(last, u[:, COLS - CY :], u[:, :CY])
        w = jnp.where(last, water[:, COLS - CY :], water[:, :CY])
        out[GROUP + 1] = jnp.broadcast_to(w, (LAYERS, CY))


def inner_kernel(*refs):
    fetched(zip(refs[:4], refs[5:9]), refs[9])
    inner_rows(*refs[5:9], refs[4])


def inner_rows(c_ref, velocity_ref, mask_ref, settling_ref, out_ref):
    water = water_of(mask_ref)

    def three(x):
        return x[:, : 2 * CY], x[:, CY : 3 * CY], x[:, 2 * CY :]

    def pick(what, layer):
        if what == "water":
            return three(water)
        if what == "c":
            return three(c_ref[:, layer, :])
        if what == "u":
            return three(velocity_ref[0, layer : layer + 1, :])
        return velocity_ref[1, layer : layer + 1, CY : 3 * CY]

    advect(pick, column(settling_ref[...]), out_ref)


def outer_kernel(
    c_ref,
    velocity_ref,
    mask_ref,
    settling_ref,
    even_ref,
    odd_ref,
    inner_ref,
    peer_ref,
    out_ref,
    both_ref,
):
    both_ref[0] = inner_ref[0]
    both_ref[1] = peer_ref[...]
    water = water_of(mask_ref)
    even = lax.axis_index("tile") % 2 == 0
    west_ref = jnp.where(even, odd_ref[...], even_ref[...])
    east_ref = jnp.where(even, even_ref[...], odd_ref[...])

    def three(west, x, east):
        return (
            jnp.concatenate([west, x[:, 2 * CY : 3 * CY]], 1),
            jnp.concatenate([x[:, :CY], x[:, 3 * CY :]], 1),
            jnp.concatenate([x[:, CY : 2 * CY], east], 1),
        )

    def pick(what, layer):
        if what == "water":
            return three(west_ref[GROUP + 1, :1, :], water, east_ref[GROUP + 1, :1, :])
        if what == "c":
            return three(west_ref[:GROUP, layer, :], c_ref[:, layer, :], east_ref[:GROUP, layer, :])
        if what == "u":
            at = slice(layer, layer + 1)
            return three(west_ref[GROUP, at, :], velocity_ref[0, at, :], east_ref[GROUP, at, :])
        v = velocity_ref[1, layer : layer + 1, :]
        return jnp.concatenate([v[:, :CY], v[:, 3 * CY :]], 1)

    advect(pick, column(settling_ref[...]), out_ref)


def gains(n, stack, table_ref, spans, first, count):
    total = [jnp.zeros((8, TILE), jnp.float32) for _ in range(count // 8)]
    for blocks in DOTS:
        base = first[blocks[0]]
        made = jnp.dot(
            table_ref[base : first[blocks[-1] + 1], :], stack, preferred_element_type=jnp.float32
        )
        for b in blocks:
            span = spans[b]
            skip = (count - span) // 8
            for ii in range(8):
                partner = n[8 * b + ii : 8 * b + ii + 1]
                for g in range(span // 8):
                    row = first[b] - base + ii * span + 8 * g
                    total[skip + g] = total[skip + g] + made[row : row + 8] * partner
    return jnp.concatenate(total, 0)


def stack_of(n):
    high, low = split(n)
    return jnp.concatenate([high, low, high, low], 0)


def react_kernel(ours_ref, theirs_ref, all_ref, own_ref, linear_ref, *rest):
    keep_ref, send_ref, whole = rest[-3:]
    lanes = whole.shape[0]
    layers = ours_ref.shape[1]
    filled = 0
    if send_ref.shape[0] > layers:
        for ref in rest[:-3]:
            send_ref[filled : filled + ref.shape[0]] = ref[...]
            filled += ref.shape[0]
    far, near = lax.axis_index("far"), lax.axis_index("near")
    groups = [2 * f + n for f in (far, 1 - far) for n in (near, 1 - near)]
    parts = [ref.at[place] for ref in (ours_ref, theirs_ref) for place in range(2)]

    def step(index, carry):
        places = []
        for k in range(lanes):
            at = index * lanes + k
            slot = at // (WIDTH // TILE)
            places.append((slot, pl.ds(pl.multiple_of((at % (WIDTH // TILE)) * TILE, TILE), TILE)))
        ns = []
        for k, (slot, at) in enumerate(places):
            for group, part in zip(groups, parts):
                whole[k, group] = part[slot, :, at]
            ns.append(whole[k].reshape(NC, TILE))
        stacks = [stack_of(n) for n in ns]
        mades = [gains(*both, all_ref, ALL_SPANS, ALL_STARTS, NC) for both in zip(ns, stacks)]
        linears = [
            jnp.dot(linear_ref[...], stack, preferred_element_type=jnp.float32) for stack in stacks
        ]
        ns = [n + (HALF_SCALE * made + linear) for n, made, linear in zip(ns, mades, linears)]
        stacks = [stack_of(n) for n in ns]
        mades = [gains(*both, own_ref, OWN_SPANS, OWN_STARTS, NC // 2) for both in zip(ns, stacks)]
        mine = linear_ref[pl.ds(pl.multiple_of(far * (NC // 2), NC // 2), NC // 2), :]
        linears = [
            jnp.dot(mine, stack, preferred_element_type=jnp.float32) for stack in stacks
        ]
        for n, made, linear, (slot, at) in zip(ns, mades, linears, places):
            n = jnp.where(far == 0, n[: NC // 2], n[NC // 2 :]) + (HALF_SCALE * made + linear)
            keep_ref[slot, :, at] = jnp.where(near == 0, n[:GROUP], n[GROUP:])
            send_ref[filled + slot, :, at] = jnp.where(near == 0, n[GROUP:], n[:GROUP])
        return carry

    lax.fori_loop(0, layers * WIDTH // (lanes * TILE), step, 0)


def react(ours, theirs, tables, later=(), earlier=()):
    layers = ours.shape[1]
    sent = layers + sum(x.shape[0] for x in earlier)
    return call(
        react_kernel,
        (f32(layers, GROUP, WIDTH), f32(sent, GROUP, WIDTH)),
        "react",
        scratch=[pltpu.VMEM((min(LANES, layers * WIDTH // TILE), 4, GROUP, TILE), jnp.float32)],
        cost=3_000_000_000 * layers,
        in_specs=[pl.BlockSpec(memory_space=pltpu.VMEM)] * (5 + len(earlier))
        + [pl.BlockSpec(memory_space=pl.ANY)] * len(later),
    )(ours, theirs, *tables, *earlier, *later)


def lay_kernel(inner_ref, first_ref, second_ref, peer_ref, out_ref):
    near = lax.axis_index("near")
    outer_refs = (first_ref, second_ref)
    for layer in range(LAYERS):
        slot = layer % 2
        mine = near == layer // 2
        inner = jnp.where(mine, inner_ref[slot], peer_ref[slot])
        outer = jnp.where(mine, outer_refs[slot][0], peer_ref[2 + slot])
        out_ref[:, layer, :] = jnp.concatenate([outer[:, :CY], inner, outer[:, CY:]], 1)


def swapped_in_pairs(x, first):
    length = lax.axis_size("tile")
    pairs = [(i, i + 1) for i in range(first, length - 1, 2)]
    return lax.ppermute(x, "tile", pairs + [(b, a) for a, b in pairs])


def swapped(x, axis):
    return lax.ppermute(x, axis, [(0, 1), (1, 0)])


def body(
    concentration,
    velocity,
    land_mask,
    settling,
    breakage_rate,
    kernel_levels,
    pair_target,
    fragment_weights,
):
    local = (
        concentration,
        velocity,
        land_mask.reshape(COLS // 128, 128),
        settling.reshape(1, GROUP),
    )
    halves = f32(2, 2, GROUP, WIDTH)
    edge = f32(GROUP + 2, LAYERS, CY)
    placed = [pltpu.with_memory_space_constraint(x, pltpu.HBM) for x in local]
    to_even, to_odd = call(
        edge_kernel,
        (edge, edge),
        "edges",
        scratch=[
            pltpu.VMEM(local[2].shape, jnp.int32),
            pltpu.VMEM((LAYERS, COLS), jnp.float32),
            pltpu.SemaphoreType.DMA((4,)),
        ],
        in_specs=[pl.BlockSpec(memory_space=pltpu.HBM)] * 3,
    )(*placed[:3])
    from_odd, from_even = swapped_in_pairs(to_odd, 1), swapped_in_pairs(to_even, 0)
    inner = call(
        inner_kernel,
        halves,
        "inner",
        scratch=[pltpu.VMEM(x.shape, x.dtype) for x in local] + [pltpu.SemaphoreType.DMA((4,))],
        in_specs=[pl.BlockSpec(memory_space=pltpu.HBM)] * 4,
    )(*placed)
    peer = swapped(inner[1], "near")
    outer, inner = call(outer_kernel, (halves, halves), "outer", cost=1_000_000_000)(
        *local, from_even, from_odd, inner, peer
    )
    inner_far = swapped(inner, "far")
    tables = make_tables(
        kernel_levels, pair_target, fragment_weights, breakage_rate, outer
    )
    outer_peer = swapped(outer[1:], "near")
    ours = [jnp.concatenate([outer[:1, k : k + 1], outer_peer[:, k : k + 1]], 0) for k in range(2)]
    theirs = [swapped(x, "far") for x in ours]
    inner, sent = react(inner, inner_far, tables, later=ours)
    first, sent_first = react(ours[0], theirs[0], tables)
    second, sent = react(ours[1], theirs[1], tables, earlier=(sent, sent_first))
    peer = swapped(sent, "near")
    return call(lay_kernel, f32(GROUP, LAYERS, COLS), "lay")(inner, first, second, peer)


def solution(mesh):
    finer = Mesh(mesh.devices.reshape(mesh.shape["tile"], 2, 2), ("tile", "far", "near"))
    cls = ("far", "near")
    placed = (
        P(cls, None, "tile"),
        P(None, None, "tile"),
        P("tile"),
        P(cls),
        P(),
        P(),
        P(),
        P(),
    )
    return jax.shard_map(
        body, mesh=finer, in_specs=placed, out_specs=P(cls, None, "tile"), check_vma=False
    )
```

```python
import jax
import jax.numpy as jnp
from jax import lax
from jax.experimental import pallas as pl
from jax.experimental.pallas import tpu as pltpu
from jax.sharding import Mesh
from jax.sharding import PartitionSpec as P

CY = 512
CX = 4
LAYERS = 4
NC = 64
GROUP = 16
COLS = CX * CY
WIDTH = 2 * CY
TILE = 512
LANES = 4
DOTS = [[0, 1, 2, 3], [4, 5, 6, 7]]
HALF_SCALE = 0.5e-05
VMEM_LIMIT = 48 * 1024 * 1024

BLOCKS = NC // 8
ALL_SPANS = [NC - 8 * b for b in range(BLOCKS)]
OWN_SPANS = [min(NC // 2, NC - 8 * b) for b in range(BLOCKS)]


def starts(spans):
    return [8 * sum(spans[:b]) for b in range(BLOCKS + 1)]


ALL_STARTS, OWN_STARTS = starts(ALL_SPANS), starts(OWN_SPANS)


def split(x):
    high = x.astype(jnp.bfloat16)
    low = (x - high.astype(jnp.float32)).astype(jnp.bfloat16)
    return high, low


def call(kernel, out_shape, name, scratch=(), limit=VMEM_LIMIT, cost=None, **specs):
    if cost is not None:
        cost = pl.CostEstimate(flops=cost, bytes_accessed=0, transcendentals=0)
    return pl.pallas_call(
        kernel,
        out_shape=out_shape,
        scratch_shapes=scratch,
        **specs,
        compiler_params=pltpu.CompilerParams(vmem_limit_bytes=limit),
        cost_estimate=cost,
        name=name,
    )


def f32(*shape):
    return jax.ShapeDtypeStruct(shape, jnp.float32)


def table_kernel(levels_ref, target_ref, weights_ref, rate_ref, all_ref, own_ref, linear_ref):
    far = lax.axis_index("far")
    levels = levels_ref[...].astype(jnp.float32)
    row = lax.broadcasted_iota(jnp.int32, (NC, NC), 0)
    col = lax.broadcasted_iota(jnp.int32, (NC, NC), 1)
    double = 2.0 * levels
    high, low = [part.astype(jnp.float32) for part in split(double)]
    weight = jnp.where(col < row, 1.0, jnp.where(col == row, 0.5, 0.0))
    lost = jnp.concatenate([high, high, low, low], 1)
    born = lost * jnp.concatenate([weight] * 4, 1)
    target = jnp.concatenate([target_ref[...]] * 4, 1)

    def rows_of(i, first, span):
        klass = lax.broadcasted_iota(jnp.int32, (span, 4 * NC), 0) + first
        gain = jnp.where(klass == target[i : i + 1], born[i : i + 1], 0.0)
        return gain - jnp.where(klass == i, lost[i : i + 1], 0.0)

    for b in range(BLOCKS):
        for i in range(8 * b, 8 * b + 8, 2):
            span = ALL_SPANS[b]
            rows = jnp.concatenate([rows_of(i, 8 * b, span), rows_of(i + 1, 8 * b, span)], 0)
            at = ALL_STARTS[b] + (i - 8 * b) * span
            all_ref[at : at + 2 * span, :] = rows.astype(jnp.bfloat16)
            span = OWN_SPANS[b]
            first = far * (NC // 2) + (NC // 2 - span)
            rows = jnp.concatenate([rows_of(i, first, span), rows_of(i + 1, first, span)], 0)
            at = OWN_STARTS[b] + (i - 8 * b) * span
            own_ref[at : at + 2 * span, :] = rows.astype(jnp.bfloat16)
    lower = jnp.where(row <= col, weights_ref[...].astype(jnp.float32), 0.0)
    rate = rate_ref[...]
    linear = lower / jnp.sum(lower, axis=0, keepdims=True) * rate
    linear = linear - jnp.where(row == col, rate, 0.0)
    high, low = split(linear)
    linear_ref[...] = jnp.concatenate([high, high, low, low], 1)


def make_tables(kernel_levels, pair_target, fragment_weights, breakage_rate):
    bf16 = jnp.bfloat16
    return call(
        table_kernel,
        (
            jax.ShapeDtypeStruct((ALL_STARTS[-1], 4 * NC), bf16),
            jax.ShapeDtypeStruct((OWN_STARTS[-1], 4 * NC), bf16),
            jax.ShapeDtypeStruct((NC, 4 * NC), bf16),
        ),
        "tables",
    )(kernel_levels, pair_target, fragment_weights, breakage_rate.reshape(1, NC))


def column(settling):
    eye = lax.broadcasted_iota(jnp.int32, (GROUP, GROUP), 0) == lax.broadcasted_iota(
        jnp.int32, (GROUP, GROUP), 1
    )
    return jnp.sum(jnp.where(eye, settling, 0.0), axis=1, keepdims=True)


def water_of(mask_ref):
    mask = mask_ref[...].astype(jnp.float32)
    return jnp.concatenate([mask[q : q + 1] for q in range(COLS // 128)], 1)


def advect(pick, sink, out_ref):
    water_west, water, water_east = pick("water", 0)
    width = water.shape[1]
    place = lax.broadcasted_iota(jnp.int32, (1, width), 1)
    half_west = 0.5 * water_west * water
    half_east = 0.5 * water * water_east
    half_y = jnp.where(place % CY == 0, 0.0, 0.5 * water * pltpu.roll(water, 1, 1))
    above = None
    near = lax.axis_index("near")
    for layer in range(LAYERS):
        west, c, east = pick("c", layer)
        u_west, u, u_east = pick("u", layer)
        v = pick("v", layer)
        low_x = (u_west + u) * half_west
        high_x = (u + u_east) * half_east
        low_y = (v + pltpu.roll(v, 1, 1)) * half_y
        plus_y, minus_y = jnp.maximum(low_y, 0.0), jnp.minimum(low_y, 0.0)
        plus_x, minus_x = jnp.maximum(low_x, 0.0), jnp.minimum(high_x, 0.0)
        to_north = pltpu.roll(plus_y, width - 1, 1)
        from_north = pltpu.roll(minus_y, width - 1, 1)
        keep = 1.0 - jnp.maximum(high_x, 0.0) + jnp.minimum(low_x, 0.0) - to_north + minus_y
        moved = (
            c * (keep - sink)
            + west * plus_x
            - east * minus_x
            + pltpu.roll(c, 1, 1) * plus_y
            - pltpu.roll(c, width - 1, 1) * from_north
        )
        if above is not None:
            moved = moved + sink * above
        above = c
        out_ref[(near + layer // 2) % 2, layer % 2] = moved


def fetched(pairs, sems):
    copies = [pltpu.make_async_copy(*pair, sems.at[k]) for k, pair in enumerate(pairs)]
    for copy in copies:
        copy.start()
    for copy in copies:
        copy.wait()


def edge_kernel(c_ref, velocity_ref, mask_ref, to_even_ref, to_odd_ref, mask, u, sems):
    even = lax.axis_index("tile") % 2
    ends = [pl.ds(pl.multiple_of(at * (COLS - CY), CY), CY) for at in (1 - even, even)]
    outs = (to_even_ref, to_odd_ref)
    pairs = [(mask_ref, mask), (velocity_ref.at[0], u)]
    pairs += [(c_ref.at[:, :, end], out.at[:GROUP]) for end, out in zip(ends, outs)]
    fetched(pairs, sems)
    water = water_of(mask)
    for out, last in zip(outs, (even == 0, even != 0)):
        out[GROUP] = jnp.where(last, u[:, COLS - CY :], u[:, :CY])
        w = jnp.where(last, water[:, COLS - CY :], water[:, :CY])
        out[GROUP + 1] = jnp.broadcast_to(w, (LAYERS, CY))


def inner_kernel(*refs):
    fetched(zip(refs[:4], refs[5:9]), refs[9])
    inner_rows(*refs[5:9], refs[4])


def inner_rows(c_ref, velocity_ref, mask_ref, settling_ref, out_ref):
    water = water_of(mask_ref)

    def three(x):
        return x[:, : 2 * CY], x[:, CY : 3 * CY], x[:, 2 * CY :]

    def pick(what, layer):
        if what == "water":
            return three(water)
        if what == "c":
            return three(c_ref[:, layer, :])
        if what == "u":
            return three(velocity_ref[0, layer : layer + 1, :])
        return velocity_ref[1, layer : layer + 1, CY : 3 * CY]

    advect(pick, column(settling_ref[...]), out_ref)


def outer_kernel(
    c_ref,
    velocity_ref,
    mask_ref,
    settling_ref,
    even_ref,
    odd_ref,
    inner_ref,
    peer_ref,
    out_ref,
    both_ref,
):
    both_ref[0] = inner_ref[0]
    both_ref[1] = peer_ref[...]
    water = water_of(mask_ref)
    even = lax.axis_index("tile") % 2 == 0
    west_ref = jnp.where(even, odd_ref[...], even_ref[...])
    east_ref = jnp.where(even, even_ref[...], odd_ref[...])

    def three(west, x, east):
        return (
            jnp.concatenate([west, x[:, 2 * CY : 3 * CY]], 1),
            jnp.concatenate([x[:, :CY], x[:, 3 * CY :]], 1),
            jnp.concatenate([x[:, CY : 2 * CY], east], 1),
        )

    def pick(what, layer):
        if what == "water":
            return three(west_ref[GROUP + 1, :1, :], water, east_ref[GROUP + 1, :1, :])
        if what == "c":
            return three(west_ref[:GROUP, layer, :], c_ref[:, layer, :], east_ref[:GROUP, layer, :])
        if what == "u":
            at = slice(layer, layer + 1)
            return three(west_ref[GROUP, at, :], velocity_ref[0, at, :], east_ref[GROUP, at, :])
        v = velocity_ref[1, layer : layer + 1, :]
        return jnp.concatenate([v[:, :CY], v[:, 3 * CY :]], 1)

    advect(pick, column(settling_ref[...]), out_ref)


def gains(n, stack, table_ref, spans, first, count):
    total = [jnp.zeros((8, TILE), jnp.float32) for _ in range(count // 8)]
    for blocks in DOTS:
        base = first[blocks[0]]
        made = jnp.dot(
            table_ref[base : first[blocks[-1] + 1], :], stack, preferred_element_type=jnp.float32
        )
        for b in blocks:
            span = spans[b]
            skip = (count - span) // 8
            for ii in range(8):
                partner = n[8 * b + ii : 8 * b + ii + 1]
                for g in range(span // 8):
                    row = first[b] - base + ii * span + 8 * g
                    total[skip + g] = total[skip + g] + made[row : row + 8] * partner
    return jnp.concatenate(total, 0)


def stack_of(n):
    high, low = split(n)
    return jnp.concatenate([high, low, high, low], 0)


def react_kernel(ours_ref, theirs_ref, all_ref, own_ref, linear_ref, *rest):
    keep_ref, send_ref, whole = rest[-3:]
    lanes = whole.shape[0]
    layers = ours_ref.shape[1]
    filled = 0
    if send_ref.shape[0] > layers:
        for ref in rest[:-3]:
            send_ref[filled : filled + ref.shape[0]] = ref[...]
            filled += ref.shape[0]
    far, near = lax.axis_index("far"), lax.axis_index("near")
    groups = [2 * f + n for f in (far, 1 - far) for n in (near, 1 - near)]
    parts = [ref.at[place] for ref in (ours_ref, theirs_ref) for place in range(2)]

    def step(index, carry):
        places = []
        for k in range(lanes):
            at = index * lanes + k
            slot = at // (WIDTH // TILE)
            places.append((slot, pl.ds(pl.multiple_of((at % (WIDTH // TILE)) * TILE, TILE), TILE)))
        ns = []
        for k, (slot, at) in enumerate(places):
            for group, part in zip(groups, parts):
                whole[k, group] = part[slot, :, at]
            ns.append(whole[k].reshape(NC, TILE))
        stacks = [stack_of(n) for n in ns]
        mades = [gains(*both, all_ref, ALL_SPANS, ALL_STARTS, NC) for both in zip(ns, stacks)]
        linears = [
            jnp.dot(linear_ref[...], stack, preferred_element_type=jnp.float32) for stack in stacks
        ]
        ns = [n + (HALF_SCALE * made + linear) for n, made, linear in zip(ns, mades, linears)]
        stacks = [stack_of(n) for n in ns]
        mades = [gains(*both, own_ref, OWN_SPANS, OWN_STARTS, NC // 2) for both in zip(ns, stacks)]
        mine = linear_ref[pl.ds(pl.multiple_of(far * (NC // 2), NC // 2), NC // 2), :]
        linears = [
            jnp.dot(mine, stack, preferred_element_type=jnp.float32) for stack in stacks
        ]
        for n, made, linear, (slot, at) in zip(ns, mades, linears, places):
            n = jnp.where(far == 0, n[: NC // 2], n[NC // 2 :]) + (HALF_SCALE * made + linear)
            keep_ref[slot, :, at] = jnp.where(near == 0, n[:GROUP], n[GROUP:])
            send_ref[filled + slot, :, at] = jnp.where(near == 0, n[GROUP:], n[:GROUP])
        return carry

    lax.fori_loop(0, layers * WIDTH // (lanes * TILE), step, 0)


def react(ours, theirs, tables, later=(), earlier=()):
    layers = ours.shape[1]
    sent = layers + sum(x.shape[0] for x in earlier)
    return call(
        react_kernel,
        (f32(layers, GROUP, WIDTH), f32(sent, GROUP, WIDTH)),
        "react",
        scratch=[pltpu.VMEM((min(LANES, layers * WIDTH // TILE), 4, GROUP, TILE), jnp.float32)],
        cost=3_000_000_000 * layers,
        in_specs=[pl.BlockSpec(memory_space=pltpu.VMEM)] * (5 + len(earlier))
        + [pl.BlockSpec(memory_space=pl.ANY)] * len(later),
    )(ours, theirs, *tables, *earlier, *later)


def lay_kernel(inner_ref, first_ref, second_ref, peer_ref, out_ref):
    near = lax.axis_index("near")
    outer_refs = (first_ref, second_ref)
    for layer in range(LAYERS):
        slot = layer % 2
        mine = near == layer // 2
        inner = jnp.where(mine, inner_ref[slot], peer_ref[slot])
        outer = jnp.where(mine, outer_refs[slot][0], peer_ref[2 + slot])
        out_ref[:, layer, :] = jnp.concatenate([outer[:, :CY], inner, outer[:, CY:]], 1)


def swapped_in_pairs(x, first):
    length = lax.axis_size("tile")
    pairs = [(i, i + 1) for i in range(first, length - 1, 2)]
    return lax.ppermute(x, "tile", pairs + [(b, a) for a, b in pairs])


def swapped(x, axis):
    return lax.ppermute(x, axis, [(0, 1), (1, 0)])


def body(
    concentration,
    velocity,
    land_mask,
    settling,
    breakage_rate,
    kernel_levels,
    pair_target,
    fragment_weights,
):
    local = (
        concentration,
        velocity,
        land_mask.reshape(COLS // 128, 128),
        settling.reshape(1, GROUP),
    )
    halves = f32(2, 2, GROUP, WIDTH)
    edge = f32(GROUP + 2, LAYERS, CY)
    placed = [pltpu.with_memory_space_constraint(x, pltpu.HBM) for x in local]
    to_even, to_odd = call(
        edge_kernel,
        (edge, edge),
        "edges",
        scratch=[
            pltpu.VMEM(local[2].shape, jnp.int32),
            pltpu.VMEM((LAYERS, COLS), jnp.float32),
            pltpu.SemaphoreType.DMA((4,)),
        ],
        in_specs=[pl.BlockSpec(memory_space=pltpu.HBM)] * 3,
    )(*placed[:3])
    from_odd, from_even = swapped_in_pairs(to_odd, 1), swapped_in_pairs(to_even, 0)
    inner = call(
        inner_kernel,
        halves,
        "inner",
        scratch=[pltpu.VMEM(x.shape, x.dtype) for x in local] + [pltpu.SemaphoreType.DMA((4,))],
        in_specs=[pl.BlockSpec(memory_space=pltpu.HBM)] * 4,
    )(*placed)
    peer = swapped(inner[1], "near")
    tables = make_tables(kernel_levels, pair_target, fragment_weights, breakage_rate)
    outer, inner = call(outer_kernel, (halves, halves), "outer", cost=1_000_000_000)(
        *local, from_even, from_odd, inner, peer
    )
    inner_far = swapped(inner, "far")
    outer_peer = swapped(outer[1:], "near")
    ours = [jnp.concatenate([outer[:1, k : k + 1], outer_peer[:, k : k + 1]], 0) for k in range(2)]
    theirs = [swapped(x, "far") for x in ours]
    inner, sent = react(inner, inner_far, tables, later=ours)
    first, sent_first = react(ours[0], theirs[0], tables)
    second, sent = react(ours[1], theirs[1], tables, earlier=(sent, sent_first))
    peer = swapped(sent, "near")
    return call(lay_kernel, f32(GROUP, LAYERS, COLS), "lay")(inner, first, second, peer)


def solution(mesh):
    finer = Mesh(mesh.devices.reshape(mesh.shape["tile"], 2, 2), ("tile", "far", "near"))
    cls = ("far", "near")
    placed = (
        P(cls, None, "tile"),
        P(None, None, "tile"),
        P("tile"),
        P(cls),
        P(),
        P(),
        P(),
        P(),
    )
    return jax.shard_map(
        body, mesh=finer, in_specs=placed, out_specs=P(cls, None, "tile"), check_vma=False
    )
```
